32 devices in a mesh: row: 4 (over y, x), col: 8 (over z, core).
Axes of the slice: x: 2, y: 2, z: 4, core: 2. Of those that a mesh axis runs over, the one named last changes fastest.
Arguments:
- inputs: bfloat16 [512, 12288], P('col', 'row'), may hold values from -6 to 6
- in_weight: bfloat16 [12288, 24576], P('row', 'col'), may hold values from -0.0546875 to 0.0546875
- in_bias: float32 [24576], P('col'), may hold values from -3 to 3
- out_weight: bfloat16 [24576, 12288], P('col', 'row'), may hold values from -0.0390625 to 0.0390625
- out_bias: float32 [12288], P('row'), may hold values from -3 to 3
- cotangent: bfloat16 [512, 12288], P('col', 'row'), may hold values from -1.5 to 1.5
Outputs:
- output: bfloat16 [512, 12288], P('col', 'row')
- input_grad: bfloat16 [512, 12288], P('col', 'row')
- in_weight_grad: bfloat16 [12288, 24576], P('row', 'col')
- out_weight_grad: bfloat16 [24576, 12288], P('col', 'row')
- in_bias_grad: float32 [24576], P('col')
- out_bias_grad: float32 [12288], P('row')
The draws below stay inside these ranges and needn't reach their ends.
All inputs are finite; a program needn't handle non-finite values.
Results may differ from the reference program's by a relative error of at most 0.0049.
Values may be sent and summed in bfloat16 or wider, within the bound.
No kernel may reach another device: no remote copies, remote signals or barrier semaphores. Data moves between devices by JAX's collectives and lax.ppermute only.
A program may use at most 192 MiB of HBM per device.

```python
import math
import jax
import jax.numpy as jnp
from jax import lax

D = 12288
FF = 24576
TOKENS = 512


def block_levels(stream_key, shape, pieces, low, high):
    factor_of, own = 1.0, jax.random.fold_in(stream_key, 6)
    for position, shards_of in pieces:
        steps = jnp.exp(jax.random.uniform(jax.random.fold_in(own, position), (shards_of,), jnp.float32, low / len(pieces), high / len(pieces)))
        factor_of = factor_of * jnp.repeat(steps, shape[position] // shards_of).reshape([-1 if axis == position else 1 for axis in range(len(shape))])
    return factor_of


def normal_values(stream_key, shape, width, bound, shards=(), held_as=jnp.bfloat16):
    factor_of = block_levels(stream_key, shape, shards, -0.22, 0.18) if shards else 1.0
    result = jax.random.normal(stream_key, shape, jnp.float32) * width * factor_of
    return jnp.minimum(jnp.maximum(result, -bound), bound).astype(held_as)


def setup_inputs(seed: int = 0) -> dict:
    keys = jax.random.split(jax.random.key(seed), 7)
    inputs = normal_values(keys[0], (TOKENS, D), 1.0, 6.0, ((0, 8), (1, 4)))
    in_weight = normal_values(keys[1], (D, FF), D ** -0.5, 0.0546875, ((0, 4), (1, 8)))
    in_bias = normal_values(keys[2], (FF,), 0.5, 3.0, ((0, 8),), jnp.float32)
    out_weight = normal_values(keys[3], (FF, D), FF ** -0.5, 0.0390625, ((0, 8), (1, 4)))
    out_bias = normal_values(keys[4], (D,), 0.5, 3.0, ((0, 4),), jnp.float32)
    cotangent = normal_values(keys[5], (TOKENS, D), 0.25, 1.5, ((0, 8), (1, 4)))
    return dict(inputs=inputs, in_weight=in_weight, in_bias=in_bias, out_weight=out_weight, out_bias=out_bias, cotangent=cotangent)


root_two_pi = math.sqrt(2.0 / math.pi)

def gelu_tanh(value):
    inner = jnp.tanh(root_two_pi * (value + 0.044715 * value * value * value))
    return 0.5 * value * (1.0 + inner)

def gelu_slope(value):
    inner = jnp.tanh(root_two_pi * (value + 0.044715 * value * value * value))
    return 0.5 * (1.0 + inner) + 0.5 * value * (1.0 - inner * inner) * root_two_pi * (1.0 + 3.0 * 0.044715 * value * value)

def reference(inputs, in_weight, in_bias, out_weight, out_bias, cotangent):
    pre_act = jnp.dot(inputs, in_weight, preferred_element_type=jnp.float32) + in_bias
    hidden = gelu_tanh(pre_act).astype(jnp.bfloat16)
    output = (jnp.dot(hidden, out_weight, preferred_element_type=jnp.float32) + out_bias).astype(jnp.bfloat16)
    hidden_grad = jnp.dot(cotangent, out_weight.T, preferred_element_type=jnp.float32)
    pre_grad = (hidden_grad * gelu_slope(pre_act)).astype(jnp.bfloat16)
    input_grad = jnp.dot(pre_grad, in_weight.T, preferred_element_type=jnp.float32).astype(jnp.bfloat16)
    in_weight_grad = jnp.dot(inputs.T, pre_grad, preferred_element_type=jnp.float32).astype(jnp.bfloat16)
    out_weight_grad = jnp.dot(hidden.T, cotangent, preferred_element_type=jnp.float32).astype(jnp.bfloat16)
    in_bias_grad = lax.optimization_barrier(jnp.sum(pre_grad.astype(jnp.float32), axis=0))
    out_bias_grad = lax.optimization_barrier(jnp.sum(cotangent.astype(jnp.float32), axis=0))
    return (output, input_grad, in_weight_grad, out_weight_grad, in_bias_grad, out_bias_grad)
```

```python
import math

import jax
import jax.numpy as jnp
from jax import lax
from jax.sharding import PartitionSpec as P

root_two_pi = math.sqrt(2.0 / math.pi)
bf16 = jnp.bfloat16
f32 = jnp.float32


def gelu_both(value):
    inner = jnp.tanh(root_two_pi * (value + 0.044715 * value * value * value))
    hidden = 0.5 * value * (1.0 + inner)
    slope = 0.5 * (1.0 + inner) + 0.5 * value * (1.0 - inner * inner) * root_two_pi * (
        1.0 + 3.0 * 0.044715 * value * value
    )
    return hidden, slope


def contract_last(left, right):
    return lax.dot_general(
        left, right, (((1,), (1,)), ((), ())), preferred_element_type=f32
    )


def contract_first(left, right):
    return lax.dot_general(
        left, right, (((0,), (0,)), ((), ())), preferred_element_type=f32
    )


def column_sum(matrix):
    ones_row = jnp.ones((matrix.shape[0],), matrix.dtype)
    return jnp.dot(ones_row, matrix, preferred_element_type=f32)


class Links:
    def __init__(self, rows, cols):
        self.rows, self.cols, self.chips = rows, cols, cols // 2
        self.phases = rows.bit_length() - 1
        ring = list(range(0, self.chips, 2)) + list(range(1, self.chips, 2))[::-1]
        self.ring_pairs = [
            (ring[i] * 2 + core, ring[(i + 1) % self.chips] * 2 + core)
            for i in range(self.chips)
            for core in range(2)
        ]
        self.core_pairs = [(i, i ^ 1) for i in range(cols)]
        self.orders = [
            [(phase + core) % self.phases for phase in range(self.phases)] for core in range(2)
        ]

    def ring(self, value):
        return lax.ppermute(value, "col", self.ring_pairs)

    def swap(self, value):
        return lax.ppermute(value, "col", self.core_pairs)

    def exchange(self, value, phase):
        pairs = [
            (row * self.cols + col, (row ^ (1 << self.orders[col % 2][phase])) * self.cols + col)
            for row in range(self.rows)
            for col in range(self.cols)
        ]
        return lax.ppermute(value, ("row", "col"), pairs)

    def flips(self, position):
        return [
            sum(
                ((position >> (self.phases - 1 - phase)) & 1) << order[phase]
                for phase in range(self.phases)
            )
            for order in self.orders
        ]

    def block_at(self, position):
        row, core = lax.axis_index("row"), lax.axis_index("col") % 2
        flip = self.flips(position)
        return row ^ jnp.where(core == 0, flip[0], flip[1])

    def position_of(self, block):
        row, core = lax.axis_index("row"), lax.axis_index("col") % 2
        table = [[0] * self.rows for _ in range(2)]
        for position in range(self.rows):
            for side in range(2):
                table[side][self.flips(position)[side]] = position
        return jnp.asarray(table, jnp.int32)[core, row ^ block]

    def relative(self, value):
        size = value.shape[0] // self.rows
        return jnp.concatenate(
            [
                lax.dynamic_slice_in_dim(value, self.block_at(k) * size, size, 0)
                for k in range(self.rows)
            ]
        )

    def arrival(self, value):
        size = value.shape[0] // self.rows
        return jnp.concatenate(
            [
                lax.dynamic_slice_in_dim(value, self.position_of(b) * size, size, 0)
                for b in range(self.rows)
            ]
        )

    def row_scatter(self, value):
        for phase in range(self.phases):
            half = value.shape[0] // 2
            got = self.exchange(value[half:].astype(bf16), phase)
            value = value[:half] + got.astype(f32)
        return value

    def row_gather(self, value):
        for phase in reversed(range(self.phases)):
            value = jnp.concatenate([value, self.exchange(value, phase)])
        return value

    def ring_gather(self, value):
        half = max(self.chips // 2, 1)
        arrivals = [value]
        for _ in range(self.chips - 1):
            arrivals.append(self.ring(arrivals[-1]))
        halves = []
        for part in (arrivals[:half], arrivals[half:]):
            mine = jnp.stack(part)
            other = self.swap(mine)
            halves.append(
                jnp.stack([mine, other], axis=1).reshape(-1, value.shape[1])
            )
        return halves

    def ring_scatter(self, halves):
        tokens = halves[0].shape[0] * 2 // self.cols
        sums = []
        for value in halves:
            value = value.reshape(self.chips // 2, 2, tokens, value.shape[1])
            got = self.swap(value[:, 1].astype(bf16))
            total = value[:, 0] + got.astype(f32)
            sums.extend(total[j] for j in range(total.shape[0]))
        total = sums[1]
        for step in range(1, self.chips):
            total = self.ring(total.astype(bf16)).astype(f32) + sums[(step + 1) % self.chips]
        return total


def per_device(links, inputs, in_weight, in_bias, out_weight, out_bias, cotangent):
    ins = [links.relative(part) for part in links.ring_gather(inputs)]
    cots = [links.relative(part) for part in links.ring_gather(cotangent)]
    hiddens, slopes, grads = [], [], []
    for part in ins:
        pre_act = links.row_scatter(jnp.dot(part, in_weight, preferred_element_type=f32))
        hidden, slope = gelu_both(pre_act + in_bias)
        hiddens.append(links.row_gather(hidden.astype(bf16)))
        slopes.append(slope)
    for part, slope in zip(cots, slopes):
        hidden_grad = links.row_scatter(contract_last(part, out_weight))
        grads.append(links.row_gather((hidden_grad * slope).astype(bf16)))
    out_sum = links.ring_scatter(
        [links.arrival(jnp.dot(part, out_weight, preferred_element_type=f32)) for part in hiddens]
    )
    output = (out_sum + out_bias).astype(bf16)
    input_grad = links.ring_scatter(
        [links.arrival(contract_last(part, in_weight)) for part in grads]
    ).astype(bf16)
    ins_all, cots_all = jnp.concatenate(ins), jnp.concatenate(cots)
    hidden_all, grad_all = jnp.concatenate(hiddens), jnp.concatenate(grads)
    in_weight_grad = contract_first(ins_all, grad_all).astype(bf16)
    out_weight_grad = contract_first(hidden_all, cots_all).astype(bf16)
    in_bias_grad = column_sum(grad_all)
    out_bias_grad = column_sum(cots_all)
    return (output, input_grad, in_weight_grad, out_weight_grad, in_bias_grad, out_bias_grad)


def solution(mesh):
    links = Links(mesh.shape["row"], mesh.shape["col"])
    in_specs = (
        P("col", "row"),
        P("row", "col"),
        P("col"),
        P("col", "row"),
        P("row"),
        P("col", "row"),
    )
    out_specs = (
        P("col", "row"),
        P("col", "row"),
        P("row", "col"),
        P("col", "row"),
        P("col"),
        P("row"),
    )

    def step(*arrays):
        return per_device(links, *arrays)

    return jax.shard_map(
        step, mesh=mesh, in_specs=in_specs, out_specs=out_specs, check_vma=False
    )
```

```python
import math

import jax
import jax.numpy as jnp
from jax import lax
from jax.experimental import pallas as pl
from jax.experimental.pallas import tpu as pltpu
from jax.sharding import PartitionSpec as P

root_two_pi = math.sqrt(2.0 / math.pi)
bf16 = jnp.bfloat16
f32 = jnp.float32


def gelu_both(value):
    inner = jnp.tanh(root_two_pi * (value + 0.044715 * value * value * value))
    hidden = 0.5 * value * (1.0 + inner)
    slope = 0.5 * (1.0 + inner) + 0.5 * value * (1.0 - inner * inner) * root_two_pi * (
        1.0 + 3.0 * 0.044715 * value * value
    )
    return hidden, slope


class Links:
    def __init__(self, rows, cols):
        self.rows, self.cols, self.chips = rows, cols, cols // 2
        self.phases = rows.bit_length() - 1
        ring = list(range(0, self.chips, 2)) + list(range(1, self.chips, 2))[::-1]
        self.ring_pairs = [
            (ring[i] * 2 + core, ring[(i + 1) % self.chips] * 2 + core)
            for i in range(self.chips)
            for core in range(2)
        ]
        self.core_pairs = [(i, i ^ 1) for i in range(cols)]
        self.orders = [
            [(phase + core) % self.phases for phase in range(self.phases)] for core in range(2)
        ]

    def ring(self, value):
        return lax.ppermute(value, "col", self.ring_pairs)

    def swap(self, value):
        return lax.ppermute(value, "col", self.core_pairs)

    def exchange(self, value, phase):
        pairs = [
            (row * self.cols + col, (row ^ (1 << self.orders[col % 2][phase])) * self.cols + col)
            for row in range(self.rows)
            for col in range(self.cols)
        ]
        return lax.ppermute(value, ("row", "col"), pairs)

    def flips(self, position):
        return [
            sum(
                ((position >> (self.phases - 1 - phase)) & 1) << order[phase]
                for phase in range(self.phases)
            )
            for order in self.orders
        ]

    def block_at(self, position):
        row, core = lax.axis_index("row"), lax.axis_index("col") % 2
        flip = self.flips(position)
        return row ^ jnp.where(core == 0, flip[0], flip[1])

    def position_of(self, block):
        flip = lax.axis_index("row") ^ block
        core = lax.axis_index("col") % 2
        place = [
            sum(((flip >> bit) & 1) << (self.phases - 1 - phase) for phase, bit in enumerate(order))
            for order in self.orders
        ]
        return jnp.where(core == 0, place[0], place[1])


def then(value, *others):
    return lax.optimization_barrier((value, *others))[0]


class Order:
    def __init__(self):
        self.token = None

    def gate(self, value):
        return value if self.token is None else then(value, self.token)

    def mark(self, *values):
        self.token = then(self.token, *values)

    def run(self, call, *operands):
        *results, self.token = call(*operands, [] if self.token is None else [self.token])
        return results


def pause(flops, after):
    def kernel(*refs):
        refs[-1][...] = jnp.zeros_like(refs[-1])

    return pl.pallas_call(
        kernel,
        in_specs=[ANY] * len(after),
        out_specs=[VMEM],
        out_shape=[TOKEN],
        compiler_params=params(1),
        name="pause",
        cost_estimate=pl.CostEstimate(flops=flops, bytes_accessed=1024, transcendentals=0),
    )(*after)


class RowSum:
    def __init__(self, links, order, keep, send):
        self.links, self.order, self.keep, self.phase = links, order, keep, 0
        self.pending = links.exchange(send, 0)

    def middle(self):
        for phase in range(1, self.links.phases):
            total = self.keep + self.order.gate(self.pending).astype(f32)
            half = total.shape[0] // 2
            self.keep, send = total[:half], total[half:].astype(bf16)
            self.order.mark(send)
            self.pending = self.links.exchange(send, phase)

    def finish(self):
        return self.keep + self.order.gate(self.pending).astype(f32)


class RowGather:
    def __init__(self, links, order, value):
        self.links, self.order, self.pieces = links, order, [value]
        order.mark(value)
        self.pending = links.exchange(value, links.phases - 1)

    def middle(self):
        for phase in reversed(range(self.links.phases - 1)):
            self.pieces.append(self.order.gate(self.pending))
            whole = jnp.concatenate(self.pieces)
            self.order.mark(whole)
            self.pending = self.links.exchange(whole, phase)

    def finish(self):
        return self.pieces + [self.order.gate(self.pending)]


class ChipSum:
    def __init__(self, links, order):
        self.links, self.order, self.sums, self.total = links, order, [], None
        self.pending = None

    def swap(self, mine, other):
        self.mine, self.other = mine, self.links.swap(self.order.gate(other))

    def add(self):
        total = self.mine + self.order.gate(self.other).astype(f32)
        count = max(self.links.chips // 2, 1)
        size = total.shape[0] // count
        self.sums.extend(total[j * size : (j + 1) * size] for j in range(count))

    def send(self):
        send = self.total.astype(bf16)
        self.order.mark(send)
        self.pending = self.links.ring(send)

    def arrive(self):
        self.got = self.order.gate(self.pending)
        self.order.mark(self.got)

    def receive(self, index):
        self.arrive()
        self.total = self.got.astype(f32) + self.sums[index]


VMEM = pl.BlockSpec(memory_space=pltpu.VMEM)
ANY = pl.BlockSpec(memory_space=pl.ANY)
SMEM = pl.BlockSpec(memory_space=pltpu.SMEM)
MIB = 2**20
TOKEN = jax.ShapeDtypeStruct((8, 128), f32)


def params(mib):
    return pltpu.CompilerParams(vmem_limit_bytes=mib * MIB)


def cost(rows, depth, columns, bytes_accessed):
    return pl.CostEstimate(
        flops=2 * rows * depth * columns, bytes_accessed=bytes_accessed, transcendentals=0
    )


def width_of(columns):
    return next(width for width in (512, 384, 256, 128) if columns % width == 0)


def stage(weight, after):
    def kernel(weight_ref, *refs):
        out_ref, token_ref, sem = refs[-3:]
        copy = pltpu.make_async_copy(weight_ref, out_ref, sem)
        copy.start()
        token_ref[...] = jnp.zeros_like(token_ref)
        copy.wait()

    return pl.pallas_call(
        kernel,
        in_specs=[ANY] * (1 + len(after)),
        out_specs=[VMEM, VMEM],
        out_shape=[pltpu.VMEM(weight.shape, weight.dtype), TOKEN],
        scratch_shapes=[pltpu.SemaphoreType.DMA],
        compiler_params=params(2),
        name="stage_weight",
        cost_estimate=pl.CostEstimate(flops=0, bytes_accessed=weight.size * 2, transcendentals=0),
    )(pltpu.with_memory_space_constraint(weight, pltpu.HBM), *after)


class Weight:
    def __init__(self, value, mode, width, last):
        self.value, self.mode, self.width, self.last = value, mode, width, last
        self.count = (value.shape[0] if last else value.shape[1]) // width
        held, kept, read = (mode == name for name in ("held", "kept", "read"))
        self.in_spec = VMEM if held else ANY
        space = pltpu.VMEM if held else pltpu.HBM
        self.operand = pltpu.with_memory_space_constraint(value, space)
        self.out_specs = [VMEM] if kept else []
        self.out_shape = [pltpu.VMEM(value.shape, value.dtype)] if kept else []
        self.scratch = [pltpu.VMEM(value.shape, value.dtype)] if read else []
        self.scratch += [] if held else [pltpu.SemaphoreType.DMA((self.count,))]
        self.limit = 14 + (value.size * 2 // MIB + 1 if read else 0)

    def place(self, weight_ref, outs):
        if self.mode == "held":
            return weight_ref, ()
        staged_ref = outs[4] if self.mode == "kept" else outs[-2]
        return staged_ref, (weight_ref, staged_ref, outs[-1])

    def copy(self, weight_ref, staged_ref, sems, step):
        start = step * self.width if isinstance(step, int) else pl.multiple_of(step * self.width, self.width)
        part = (pl.ds(start, self.width), slice(None))
        part = part if self.last else part[::-1]
        return pltpu.make_async_copy(weight_ref.at[part], staged_ref.at[part], sems.at[step])

    def begin(self, route):
        for step in range(self.count if route else 0):
            self.copy(*route, step).start()

    def wait(self, step, route):
        if route:
            self.copy(*route, step).wait()


def product(left, weight_ref, start, width, last):
    if last:
        return lax.dot_general(
            left, weight_ref[pl.ds(start, width), :], (((1,), (1,)), ((), ())),
            preferred_element_type=f32,
        )
    return jnp.dot(left, weight_ref[:, pl.ds(start, width)], preferred_element_type=f32)


def to_send(links, units, rows, weight, mode, last, after):
    first, size = rows
    depth = units[0].shape[1]
    tokens = size * len(units)
    block = tokens // links.rows
    columns = weight.shape[0] if last else weight.shape[1]
    width = width_of(columns)
    source = Weight(weight, mode, width, last)

    def kernel(*refs):
        unit_refs, weight_ref = refs[: len(units)], refs[len(units)]
        outs = refs[len(units) + 1 + len(after) :]
        left_out, keep_ref, send_ref, token_ref = outs[:4]
        staged_ref, route = source.place(weight_ref, outs)
        left_ref, sem = outs[4 + len(source.out_specs) :][:2]
        source.begin(route)
        for index, unit_ref in enumerate(unit_refs):
            at, within = divmod(index * size, block)
            row = pl.multiple_of(links.position_of(at) * block + within, size)
            left_ref[pl.ds(row, size), :] = unit_ref[first : first + size, :]
        token_ref[...] = jnp.zeros_like(token_ref)
        copy = pltpu.make_async_copy(left_ref, left_out, sem)
        copy.start()

        @pl.loop(0, columns // width)
        def _(step):
            source.wait(step, route)
            start = pl.multiple_of(step * width, width)
            result = product(left_ref[...], staged_ref, start, width, last)
            keep_ref[:, pl.ds(start, width)] = result[: tokens // 2]
            send_ref[:, pl.ds(start, width)] = result[tokens // 2 :].astype(bf16)

        copy.wait()

    half = (tokens // 2, columns)
    left, keep, send, token, *copied = pl.pallas_call(
        kernel,
        in_specs=[VMEM] * len(units) + [source.in_spec] + [ANY] * len(after),
        out_specs=[ANY] + [VMEM] * 3 + source.out_specs,
        out_shape=[
            pltpu.HBM((tokens, depth), bf16),
            jax.ShapeDtypeStruct(half, f32),
            jax.ShapeDtypeStruct(half, bf16),
            TOKEN,
        ]
        + source.out_shape,
        scratch_shapes=[pltpu.VMEM((tokens, depth), bf16), pltpu.SemaphoreType.DMA] + source.scratch,
        compiler_params=params(source.limit),
        name="product_to_send",
        cost_estimate=cost(tokens, depth, columns, 8 * MIB),
    )(*units, source.operand, *after)
    return left, keep, send, (copied + [weight])[0], token


def to_scatter(links, pieces, weight, mode, last, after):
    tokens = sum(piece.shape[0] for piece in pieces)
    block, depth = pieces[0].shape
    size = tokens * 2 // links.cols
    columns = weight.shape[0] if last else weight.shape[1]
    width = width_of(columns)
    source = Weight(weight, mode, width, last)

    def kernel(*refs):
        piece_refs, weight_ref = refs[: len(pieces)], refs[len(pieces)]
        outs = refs[len(pieces) + 1 + len(after) :]
        left_out, mine_ref, other_ref, token_ref = outs[:4]
        staged_ref, route = source.place(weight_ref, outs)
        left_ref, result_ref, sem = outs[4 + len(source.out_specs) :][:3]
        source.begin(route)
        row = 0
        for piece_ref in piece_refs:
            left_ref[row : row + piece_ref.shape[0], :] = piece_ref[...]
            row += piece_ref.shape[0]
        token_ref[...] = jnp.zeros_like(token_ref)
        copy = pltpu.make_async_copy(left_ref, left_out, sem)
        copy.start()

        @pl.loop(0, columns // width)
        def _(step):
            source.wait(step, route)
            start = pl.multiple_of(step * width, width)
            result_ref[...] = product(left_ref[...], staged_ref, start, width, last)
            for unit in range(tokens // size):
                at, within = divmod(unit * size, block)
                row = pl.multiple_of(links.position_of(at) * block + within, size)
                value = result_ref[pl.ds(row, size), :]
                to = slice(unit // 2 * size, (unit // 2 + 1) * size)
                if unit % 2:
                    other_ref[to, pl.ds(start, width)] = value.astype(bf16)
                else:
                    mine_ref[to, pl.ds(start, width)] = value

        copy.wait()

    half = (tokens // 2, columns)
    left, mine, other, token, *copied = pl.pallas_call(
        kernel,
        in_specs=[VMEM] * len(pieces) + [source.in_spec] + [ANY] * len(after),
        out_specs=[ANY] + [VMEM] * 3 + source.out_specs,
        out_shape=[
            pltpu.HBM((tokens, depth), bf16),
            jax.ShapeDtypeStruct(half, f32),
            jax.ShapeDtypeStruct(half, bf16),
            TOKEN,
        ]
        + source.out_shape,
        scratch_shapes=[
            pltpu.VMEM((tokens, depth), bf16),
            pltpu.VMEM((tokens, width), f32),
            pltpu.SemaphoreType.DMA,
        ]
        + source.scratch,
        compiler_params=params(source.limit),
        name="product_to_scatter",
        cost_estimate=cost(tokens, depth, columns, 8 * MIB),
    )(*pieces, source.operand, *after)
    return left, mine, other, (copied + [weight])[0], token


def weight_grad(lefts, rights, part, base, after):
    tokens, rows = lefts[0].shape
    columns = rights[0].shape[1]
    width = width_of(rows // 2)
    steps = rows // 2 // width
    count = len(lefts)

    def kernel(*refs):
        left_refs, right_refs = refs[:count], refs[count : 2 * count]
        out_ref, token_ref = refs[-3], refs[-1]

        @pl.when(pl.program_id(0) == 0)
        def _():
            ones = jnp.ones((16, tokens), bf16)
            total = sum(jnp.dot(ones, ref[...], preferred_element_type=f32) for ref in right_refs)
            refs[-2][...] = total[:8]
            token_ref[...] = jnp.zeros_like(token_ref)

        total = sum(
            lax.dot_general(
                left[...], right[...], (((0,), (0,)), ((), ())), preferred_element_type=f32
            )
            for left, right in zip(left_refs, right_refs)
        )
        out_ref[...] = total.astype(bf16)

    extra = list(after) + ([] if base is None else [base])
    out, sums, token = pl.pallas_call(
        kernel,
        grid=(steps,),
        in_specs=[pl.BlockSpec((tokens, width), lambda i: (0, i + part * steps))] * count
        + [pl.BlockSpec((tokens, columns), lambda i: (0, 0), pipeline_mode=pl.Buffered(1))] * count
        + [ANY] * len(extra),
        out_specs=[
            pl.BlockSpec((width, columns), lambda i: (i + part * steps, 0)),
            pl.BlockSpec((8, columns), lambda i: (0, 0)),
            pl.BlockSpec((8, 128), lambda i: (0, 0)),
        ],
        out_shape=[
            jax.ShapeDtypeStruct((rows, columns), bf16),
            jax.ShapeDtypeStruct((8, columns), f32),
            TOKEN,
        ],
        input_output_aliases={} if base is None else {2 * count + len(after): 0},
        compiler_params=params(24),
        name="weight_grad",
        cost_estimate=cost(rows // 2, count * tokens, columns, rows * columns),
    )(*lefts, *rights, *extra)
    return out, sums[0], token


def per_device(links, inputs, in_weight, in_bias, out_weight, out_bias, cotangent):
    half, chips = max(links.chips // 2, 1), links.chips
    order = Order()
    whole = (0, inputs.shape[0])

    def bring(arrivals, swaps, pending, count):
        for _ in range(count):
            value = order.gate(pending)
            order.mark(value)
            arrivals.append(value)
            pending = links.ring(value) if len(arrivals) < chips else None
            swaps.append(links.swap(value))
        return pending

    def units(arrivals, swapped, part):
        chosen = slice(part * half, (part + 1) * half)
        return [u for pair in zip(arrivals[chosen], swapped[chosen]) for u in pair]

    ins, cots = [inputs], [cotangent]
    next_in, next_cot = links.ring(inputs), links.ring(cotangent)
    in_swaps, cot_swaps = [links.swap(inputs)], [links.swap(cotangent)]
    (staged,) = order.run(stage, in_weight)
    next_in = bring(ins, in_swaps, next_in, half - 1)
    left_in0, keep, send, _ = order.run(
        to_send, links, units(ins, in_swaps, 0), whole, staged, "held", False
    )
    sum_p0 = RowSum(links, order, keep, send)
    next_cot = bring(cots, cot_swaps, next_cot, half - 1)
    left_cot0, keep, send, _ = order.run(
        to_send, links, units(cots, cot_swaps, 0), whole, out_weight, "read", True
    )
    sum_g0 = RowSum(links, order, keep, send)
    sum_p0.middle()
    next_in = bring(ins, in_swaps, next_in, half - 1)
    hidden, slope0 = gelu_both(sum_p0.finish() + in_bias)
    hid0 = RowGather(links, order, hidden.astype(bf16))
    sum_g0.middle()
    next_cot = bring(cots, cot_swaps, next_cot, half - 1)
    hid0.middle()
    bring(ins, in_swaps, next_in, 1)
    left_in1, keep, send, _ = order.run(
        to_send, links, units(ins, in_swaps, 1), whole, in_weight, "read", False
    )
    sum_p1 = RowSum(links, order, keep, send)
    grad0 = RowGather(links, order, (sum_g0.finish() * slope0).astype(bf16))
    bring(cots, cot_swaps, next_cot, 1)
    grad0.middle()
    left_cot1, keep, send, staged = order.run(
        to_send, links, units(cots, cot_swaps, 1), whole, out_weight, "kept", True
    )
    sum_g1 = RowSum(links, order, keep, send)
    sum_p1.middle()
    left_hid0, mine, other, _ = order.run(to_scatter, links, hid0.finish(), staged, "held", False)
    hidden, slope1 = gelu_both(sum_p1.finish() + in_bias)
    hid1 = RowGather(links, order, hidden.astype(bf16))
    outs = ChipSum(links, order)
    outs.swap(mine, other)
    grads0 = grad0.finish()
    order.mark(grads0[-1])
    left_grad0, mine, other, _ = order.run(to_scatter, links, grads0, in_weight, "read", True)
    hid1.middle()
    sum_g1.middle()
    outs.add()
    outs.total = outs.sums[1]
    for index in range(2, half):
        outs.send()
        outs.receive(index)
    outs.send()
    igs = ChipSum(links, order)
    igs.swap(mine, other)
    grad1 = RowGather(links, order, (sum_g1.finish() * slope1).astype(bf16))
    left_hid1, mine, other, _ = order.run(to_scatter, links, hid1.finish(), staged, "held", False)
    grad1.middle()
    outs.arrive()
    outs.swap(mine, other)
    igs.add()
    igs.total = igs.sums[1]
    for index in range(2, half):
        igs.send()
        igs.receive(index)
    igs.send()
    hids, cot_lefts = [left_hid0, left_hid1], [left_cot0, left_cot1]
    partial, out_bias_grad = order.run(weight_grad, hids, cot_lefts, 0, None)
    grads1 = grad1.finish()
    order.mark(grads1[-1])
    outs.add()
    outs.total = outs.got.astype(f32) + outs.sums[half]
    outs.send()
    left_grad1, mine, other, _ = order.run(to_scatter, links, grads1, in_weight, "read", True)
    igs.arrive()
    igs.swap(mine, other)
    for index in range(half + 1, chips):
        outs.receive(index)
        outs.send()
    igs.add()
    igs.total = igs.got.astype(f32) + igs.sums[half]
    igs.send()
    out_weight_grad, _ = order.run(weight_grad, hids, cot_lefts, 1, partial)
    outs.receive(0)
    in_lefts, grads = [left_in0, left_in1], [left_grad0, left_grad1]
    partial, in_bias_grad = order.run(weight_grad, in_lefts, grads, 0, None)
    for index in range(half + 1, chips):
        igs.receive(index)
        igs.send()
    in_weight_grad, _ = order.run(weight_grad, in_lefts, grads, 1, partial)
    igs.receive(0)

    output = (outs.total + out_bias).astype(bf16)
    input_grad = igs.total.astype(bf16)
    return (output, input_grad, in_weight_grad, out_weight_grad, in_bias_grad, out_bias_grad)


def solution(mesh):
    links = Links(mesh.shape["row"], mesh.shape["col"])
    in_specs = (
        P("col", "row"),
        P("row", "col"),
        P("col"),
        P("col", "row"),
        P("row"),
        P("col", "row"),
    )
    out_specs = (
        P("col", "row"),
        P("col", "row"),
        P("row", "col"),
        P("col", "row"),
        P("col"),
        P("row"),
    )

    def step(*arrays):
        return per_device(links, *arrays)

    return jax.shard_map(
        step, mesh=mesh, in_specs=in_specs, out_specs=out_specs, check_vma=False
    )
```

```python
import math

import jax
import jax.numpy as jnp
from jax import lax
from jax.experimental import pallas as pl
from jax.experimental.pallas import tpu as pltpu
from jax.sharding import PartitionSpec as P

root_two_pi = math.sqrt(2.0 / math.pi)
bf16 = jnp.bfloat16
f32 = jnp.float32


def gelu_both(value):
    inner = jnp.tanh(root_two_pi * (value + 0.044715 * value * value * value))
    hidden = 0.5 * value * (1.0 + inner)
    slope = 0.5 * (1.0 + inner) + 0.5 * value * (1.0 - inner * inner) * root_two_pi * (
        1.0 + 3.0 * 0.044715 * value * value
    )
    return hidden, slope


class Links:
    def __init__(self, rows, cols):
        self.rows, self.cols, self.chips = rows, cols, cols // 2
        self.phases = rows.bit_length() - 1
        ring = list(range(0, self.chips, 2)) + list(range(1, self.chips, 2))[::-1]
        self.ring_pairs = [
            (ring[i] * 2 + core, ring[(i + 1) % self.chips] * 2 + core)
            for i in range(self.chips)
            for core in range(2)
        ]
        self.core_pairs = [(i, i ^ 1) for i in range(cols)]
        self.orders = [
            [(phase + core) % self.phases for phase in range(self.phases)] for core in range(2)
        ]

    def ring(self, value):
        return lax.ppermute(value, "col", self.ring_pairs)

    def swap(self, value):
        return lax.ppermute(value, "col", self.core_pairs)

    def exchange(self, value, phase):
        pairs = [
            (row * self.cols + col, (row ^ (1 << self.orders[col % 2][phase])) * self.cols + col)
            for row in range(self.rows)
            for col in range(self.cols)
        ]
        return lax.ppermute(value, ("row", "col"), pairs)

    def flips(self, position):
        return [
            sum(
                ((position >> (self.phases - 1 - phase)) & 1) << order[phase]
                for phase in range(self.phases)
            )
            for order in self.orders
        ]

    def block_at(self, position):
        row, core = lax.axis_index("row"), lax.axis_index("col") % 2
        flip = self.flips(position)
        return row ^ jnp.where(core == 0, flip[0], flip[1])

    def position_of(self, block):
        flip = lax.axis_index("row") ^ block
        core = lax.axis_index("col") % 2
        place = [
            sum(((flip >> bit) & 1) << (self.phases - 1 - phase) for phase, bit in enumerate(order))
            for order in self.orders
        ]
        return jnp.where(core == 0, place[0], place[1])


def then(value, *others):
    return lax.optimization_barrier((value, *others))[0]


class Order:
    def __init__(self):
        self.token = None

    def gate(self, value):
        return value if self.token is None else then(value, self.token)

    def mark(self, *values):
        self.token = then(self.token, *values)

    def run(self, call, *operands):
        *results, self.token = call(*operands, [] if self.token is None else [self.token])
        return results


def pause(flops, after):
    def kernel(*refs):
        refs[-1][...] = jnp.zeros_like(refs[-1])

    return pl.pallas_call(
        kernel,
        in_specs=[ANY] * len(after),
        out_specs=[VMEM],
        out_shape=[TOKEN],
        compiler_params=params(1),
        name="pause",
        cost_estimate=pl.CostEstimate(flops=flops, bytes_accessed=1024, transcendentals=0),
    )(*after)


class RowSum:
    def __init__(self, links, order, keep, send):
        self.links, self.order, self.keep, self.phase = links, order, keep, 0
        self.pending = links.exchange(send, 0)

    def middle(self):
        for phase in range(1, self.links.phases):
            total = self.keep + self.order.gate(self.pending).astype(f32)
            half = total.shape[0] // 2
            self.keep, send = total[:half], total[half:].astype(bf16)
            self.order.mark(send)
            self.pending = self.links.exchange(send, phase)

    def finish(self):
        return self.keep + self.order.gate(self.pending).astype(f32)


class RowGather:
    def __init__(self, links, order, value):
        self.links, self.order, self.pieces = links, order, [value]
        order.mark(value)
        self.pending = links.exchange(value, links.phases - 1)

    def middle(self):
        for phase in reversed(range(self.links.phases - 1)):
            self.pieces.append(self.order.gate(self.pending))
            whole = jnp.concatenate(self.pieces)
            self.order.mark(whole)
            self.pending = self.links.exchange(whole, phase)

    def finish(self):
        return self.pieces + [self.order.gate(self.pending)]


class ChipSum:
    def __init__(self, links, order):
        self.links, self.order, self.sums, self.total = links, order, [], None
        self.pending = None

    def swap(self, mine, other):
        self.mine, self.other = mine, self.links.swap(self.order.gate(other))

    def add(self):
        total = self.mine + self.order.gate(self.other).astype(f32)
        count = max(self.links.chips // 2, 1)
        size = total.shape[0] // count
        self.sums.extend(total[j * size : (j + 1) * size] for j in range(count))

    def send(self):
        send = self.total.astype(bf16)
        self.order.mark(send)
        self.pending = self.links.ring(send)

    def arrive(self):
        self.got = self.order.gate(self.pending)
        self.order.mark(self.got)

    def receive(self, index):
        self.arrive()
        self.total = self.got.astype(f32) + self.sums[index]


VMEM = pl.BlockSpec(memory_space=pltpu.VMEM)
ANY = pl.BlockSpec(memory_space=pl.ANY)
SMEM = pl.BlockSpec(memory_space=pltpu.SMEM)
MIB = 2**20
TOKEN = jax.ShapeDtypeStruct((8, 128), f32)


def params(mib):
    return pltpu.CompilerParams(vmem_limit_bytes=mib * MIB)


def cost(rows, depth, columns, bytes_accessed):
    return pl.CostEstimate(
        flops=2 * rows * depth * columns, bytes_accessed=bytes_accessed, transcendentals=0
    )


def width_of(columns):
    return next(width for width in (512, 384, 256, 128) if columns % width == 0)


def stage(weight, after):
    def kernel(weight_ref, *refs):
        out_ref, token_ref, sem = refs[-3:]
        copy = pltpu.make_async_copy(weight_ref, out_ref, sem)
        copy.start()
        token_ref[...] = jnp.zeros_like(token_ref)
        copy.wait()

    return pl.pallas_call(
        kernel,
        in_specs=[ANY] * (1 + len(after)),
        out_specs=[VMEM, VMEM],
        out_shape=[pltpu.VMEM(weight.shape, weight.dtype), TOKEN],
        scratch_shapes=[pltpu.SemaphoreType.DMA],
        compiler_params=params(2),
        name="stage_weight",
        cost_estimate=pl.CostEstimate(flops=0, bytes_accessed=weight.size * 2, transcendentals=0),
    )(pltpu.with_memory_space_constraint(weight, pltpu.HBM), *after)


class Weight:
    def __init__(self, value, mode, width, last):
        self.value, self.mode, self.width, self.last = value, mode, width, last
        self.count = (value.shape[0] if last else value.shape[1]) // width
        held, kept, read = (mode == name for name in ("held", "kept", "read"))
        self.in_spec = VMEM if held else ANY
        space = pltpu.VMEM if held else pltpu.HBM
        self.operand = pltpu.with_memory_space_constraint(value, space)
        self.out_specs = [VMEM] if kept else []
        self.out_shape = [pltpu.VMEM(value.shape, value.dtype)] if kept else []
        self.scratch = [pltpu.VMEM(value.shape, value.dtype)] if read else []
        self.scratch += [] if held else [pltpu.SemaphoreType.DMA((self.count,))]
        self.limit = 14 + (value.size * 2 // MIB + 1 if read else 0)

    def place(self, weight_ref, outs):
        if self.mode == "held":
            return weight_ref, ()
        staged_ref = outs[4] if self.mode == "kept" else outs[-2]
        return staged_ref, (weight_ref, staged_ref, outs[-1])

    def copy(self, weight_ref, staged_ref, sems, step):
        start = step * self.width if isinstance(step, int) else pl.multiple_of(step * self.width, self.width)
        part = (pl.ds(start, self.width), slice(None))
        part = part if self.last else part[::-1]
        return pltpu.make_async_copy(weight_ref.at[part], staged_ref.at[part], sems.at[step])

    def begin(self, route):
        for step in range(self.count if route else 0):
            self.copy(*route, step).start()

    def wait(self, step, route):
        if route:
            self.copy(*route, step).wait()


def product(left, weight_ref, start, width, last):
    if last:
        return lax.dot_general(
            left, weight_ref[pl.ds(start, width), :], (((1,), (1,)), ((), ())),
            preferred_element_type=f32,
        )
    return jnp.dot(left, weight_ref[:, pl.ds(start, width)], preferred_element_type=f32)


def to_send(links, units, rows, weight, mode, last, after):
    first, size = rows
    depth = units[0].shape[1]
    tokens = size * len(units)
    block = tokens // links.rows
    columns = weight.shape[0] if last else weight.shape[1]
    width = width_of(columns)
    source = Weight(weight, mode, width, last)

    def kernel(*refs):
        unit_refs, weight_ref = refs[: len(units)], refs[len(units)]
        outs = refs[len(units) + 1 + len(after) :]
        left_out, keep_ref, send_ref, token_ref = outs[:4]
        staged_ref, route = source.place(weight_ref, outs)
        left_ref, sem = outs[4 + len(source.out_specs) :][:2]
        source.begin(route)
        for index, unit_ref in enumerate(unit_refs):
            at, within = divmod(index * size, block)
            row = pl.multiple_of(links.position_of(at) * block + within, size)
            left_ref[pl.ds(row, size), :] = unit_ref[first : first + size, :]
        token_ref[...] = jnp.zeros_like(token_ref)
        copy = pltpu.make_async_copy(left_ref, left_out, sem)
        copy.start()

        @pl.loop(0, columns // width)
        def _(step):
            source.wait(step, route)
            start = pl.multiple_of(step * width, width)
            result = product(left_ref[...], staged_ref, start, width, last)
            keep_ref[:, pl.ds(start, width)] = result[: tokens // 2]
            send_ref[:, pl.ds(start, width)] = result[tokens // 2 :].astype(bf16)

        copy.wait()

    half = (tokens // 2, columns)
    left, keep, send, token, *copied = pl.pallas_call(
        kernel,
        in_specs=[VMEM] * len(units) + [source.in_spec] + [ANY] * len(after),
        out_specs=[ANY] + [VMEM] * 3 + source.out_specs,
        out_shape=[
            pltpu.HBM((tokens, depth), bf16),
            jax.ShapeDtypeStruct(half, f32),
            jax.ShapeDtypeStruct(half, bf16),
            TOKEN,
        ]
        + source.out_shape,
        scratch_shapes=[pltpu.VMEM((tokens, depth), bf16), pltpu.SemaphoreType.DMA] + source.scratch,
        compiler_params=params(source.limit),
        name="product_to_send",
        cost_estimate=cost(tokens, depth, columns, 8 * MIB),
    )(*units, source.operand, *after)
    return left, keep, send, (copied + [weight])[0], token


def to_scatter(links, pieces, weight, mode, last, after):
    tokens = sum(piece.shape[0] for piece in pieces)
    block, depth = pieces[0].shape
    size = tokens * 2 // links.cols
    columns = weight.shape[0] if last else weight.shape[1]
    width = width_of(columns)
    source = Weight(weight, mode, width, last)

    def kernel(*refs):
        piece_refs, weight_ref = refs[: len(pieces)], refs[len(pieces)]
        outs = refs[len(pieces) + 1 + len(after) :]
        left_out, mine_ref, other_ref, token_ref = outs[:4]
        staged_ref, route = source.place(weight_ref, outs)
        left_ref, result_ref, sem = outs[4 + len(source.out_specs) :][:3]
        source.begin(route)
        row = 0
        for piece_ref in piece_refs:
            left_ref[row : row + piece_ref.shape[0], :] = piece_ref[...]
            row += piece_ref.shape[0]
        token_ref[...] = jnp.zeros_like(token_ref)
        copy = pltpu.make_async_copy(left_ref, left_out, sem)
        copy.start()

        @pl.loop(0, columns // width)
        def _(step):
            source.wait(step, route)
            start = pl.multiple_of(step * width, width)
            result_ref[...] = product(left_ref[...], staged_ref, start, width, last)
            for unit in range(tokens // size):
                at, within = divmod(unit * size, block)
                row = pl.multiple_of(links.position_of(at) * block + within, size)
                value = result_ref[pl.ds(row, size), :]
                to = slice(unit // 2 * size, (unit // 2 + 1) * size)
                if unit % 2:
                    other_ref[to, pl.ds(start, width)] = value.astype(bf16)
                else:
                    mine_ref[to, pl.ds(start, width)] = value

        copy.wait()

    half = (tokens // 2, columns)
    left, mine, other, token, *copied = pl.pallas_call(
        kernel,
        in_specs=[VMEM] * len(pieces) + [source.in_spec] + [ANY] * len(after),
        out_specs=[ANY] + [VMEM] * 3 + source.out_specs,
        out_shape=[
            pltpu.HBM((tokens, depth), bf16),
            jax.ShapeDtypeStruct(half, f32),
            jax.ShapeDtypeStruct(half, bf16),
            TOKEN,
        ]
        + source.out_shape,
        scratch_shapes=[
            pltpu.VMEM((tokens, depth), bf16),
            pltpu.VMEM((tokens, width), f32),
            pltpu.SemaphoreType.DMA,
        ]
        + source.scratch,
        compiler_params=params(source.limit),
        name="product_to_scatter",
        cost_estimate=cost(tokens, depth, columns, 8 * MIB),
    )(*pieces, source.operand, *after)
    return left, mine, other, (copied + [weight])[0], token


def weight_grad(lefts, rights, part, base, after):
    tokens, rows = lefts[0].shape
    columns = rights[0].shape[1]
    width = width_of(rows // 2)
    steps = rows // 2 // width
    count = len(lefts)

    def kernel(*refs):
        left_refs, right_refs = refs[:count], refs[count : 2 * count]
        out_ref, token_ref = refs[-3], refs[-1]

        @pl.when(pl.program_id(0) == 0)
        def _():
            if part == 0:
                ones = jnp.ones((16, tokens), bf16)
                total = sum(
                    jnp.dot(ones, ref[...], preferred_element_type=f32) for ref in right_refs
                )
                refs[-2][...] = total[:8]
            else:
                refs[-2][...] = jnp.zeros_like(refs[-2])
            token_ref[...] = jnp.zeros_like(token_ref)

        total = sum(
            lax.dot_general(
                left[...], right[...], (((0,), (0,)), ((), ())), preferred_element_type=f32
            )
            for left, right in zip(left_refs, right_refs)
        )
        out_ref[...] = total.astype(bf16)

    extra = list(after) + ([] if base is None else [base])
    out, sums, token = pl.pallas_call(
        kernel,
        grid=(steps,),
        in_specs=[pl.BlockSpec((tokens, width), lambda i: (0, i + part * steps))] * count
        + [pl.BlockSpec((tokens, columns), lambda i: (0, 0), pipeline_mode=pl.Buffered(1))] * count
        + [ANY] * len(extra),
        out_specs=[
            pl.BlockSpec((width, columns), lambda i: (i + part * steps, 0)),
            pl.BlockSpec((8, columns), lambda i: (0, 0)),
            pl.BlockSpec((8, 128), lambda i: (0, 0)),
        ],
        out_shape=[
            jax.ShapeDtypeStruct((rows, columns), bf16),
            jax.ShapeDtypeStruct((8, columns), f32),
            TOKEN,
        ],
        input_output_aliases={} if base is None else {2 * count + len(after): 0},
        compiler_params=params(24),
        name="weight_grad",
        cost_estimate=cost(rows // 2, count * tokens, columns, rows * columns),
    )(*lefts, *rights, *extra)
    return out, sums[0], token


def per_device(links, inputs, in_weight, in_bias, out_weight, out_bias, cotangent):
    half, chips = max(links.chips // 2, 1), links.chips
    order = Order()
    whole = (0, inputs.shape[0])

    def bring(arrivals, swaps, pending, count):
        for _ in range(count):
            value = order.gate(pending)
            order.mark(value)
            arrivals.append(value)
            pending = links.ring(value) if len(arrivals) < chips else None
            swaps.append(links.swap(value))
        return pending

    def units(arrivals, swapped, part):
        chosen = slice(part * half, (part + 1) * half)
        return [u for pair in zip(arrivals[chosen], swapped[chosen]) for u in pair]

    ins, cots = [inputs], [cotangent]
    next_in, next_cot = links.ring(inputs), links.ring(cotangent)
    in_swaps, cot_swaps = [links.swap(inputs)], [links.swap(cotangent)]
    (staged,) = order.run(stage, in_weight)
    next_in = bring(ins, in_swaps, next_in, half - 1)
    left_in0, keep, send, _ = order.run(
        to_send, links, units(ins, in_swaps, 0), whole, staged, "held", False
    )
    sum_p0 = RowSum(links, order, keep, send)
    next_cot = bring(cots, cot_swaps, next_cot, half - 1)
    left_cot0, keep, send, _ = order.run(
        to_send, links, units(cots, cot_swaps, 0), whole, out_weight, "read", True
    )
    sum_g0 = RowSum(links, order, keep, send)
    sum_p0.middle()
    next_in = bring(ins, in_swaps, next_in, half - 1)
    hidden, slope0 = gelu_both(sum_p0.finish() + in_bias)
    hid0 = RowGather(links, order, hidden.astype(bf16))
    sum_g0.middle()
    next_cot = bring(cots, cot_swaps, next_cot, half - 1)
    hid0.middle()
    bring(ins, in_swaps, next_in, 1)
    left_in1, keep, send, _ = order.run(
        to_send, links, units(ins, in_swaps, 1), whole, in_weight, "read", False
    )
    sum_p1 = RowSum(links, order, keep, send)
    grad0 = RowGather(links, order, (sum_g0.finish() * slope0).astype(bf16))
    bring(cots, cot_swaps, next_cot, 1)
    grad0.middle()
    left_cot1, keep, send, staged = order.run(
        to_send, links, units(cots, cot_swaps, 1), whole, out_weight, "kept", True
    )
    sum_g1 = RowSum(links, order, keep, send)
    sum_p1.middle()
    left_hid0, mine, other, _ = order.run(to_scatter, links, hid0.finish(), staged, "held", False)
    hidden, slope1 = gelu_both(sum_p1.finish() + in_bias)
    hid1 = RowGather(links, order, hidden.astype(bf16))
    outs = ChipSum(links, order)
    outs.swap(mine, other)
    grads0 = grad0.finish()
    order.mark(grads0[-1])
    left_grad0, mine, other, _ = order.run(to_scatter, links, grads0, in_weight, "read", True)
    hid1.middle()
    sum_g1.middle()
    outs.add()
    outs.total = outs.sums[1]
    for index in range(2, half):
        outs.send()
        outs.receive(index)
    outs.send()
    igs = ChipSum(links, order)
    igs.swap(mine, other)
    grad1 = RowGather(links, order, (sum_g1.finish() * slope1).astype(bf16))
    left_hid1, mine, other, _ = order.run(to_scatter, links, hid1.finish(), staged, "held", False)
    grad1.middle()
    outs.arrive()
    outs.swap(mine, other)
    igs.add()
    igs.total = igs.sums[1]
    for index in range(2, half):
        igs.send()
        igs.receive(index)
    igs.send()
    hids, cot_lefts = [left_hid0, left_hid1], [left_cot0, left_cot1]
    partial, out_bias_grad = order.run(weight_grad, hids, cot_lefts, 0, None)
    grads1 = grad1.finish()
    order.mark(grads1[-1])
    outs.add()
    outs.total = outs.got.astype(f32) + outs.sums[half]
    outs.send()
    left_grad1, mine, other, _ = order.run(to_scatter, links, grads1, in_weight, "read", True)
    igs.arrive()
    igs.swap(mine, other)
    for index in range(half + 1, chips):
        outs.receive(index)
        outs.send()
    igs.add()
    igs.total = igs.got.astype(f32) + igs.sums[half]
    igs.send()
    out_weight_grad, _ = order.run(weight_grad, hids, cot_lefts, 1, partial)
    outs.receive(0)
    in_lefts, grads = [left_in0, left_in1], [left_grad0, left_grad1]
    partial, in_bias_grad = order.run(weight_grad, in_lefts, grads, 0, None)
    for index in range(half + 1, chips):
        igs.receive(index)
        igs.send()
    in_weight_grad, _ = order.run(weight_grad, in_lefts, grads, 1, partial)
    igs.receive(0)

    output = (outs.total + out_bias).astype(bf16)
    input_grad = igs.total.astype(bf16)
    return (output, input_grad, in_weight_grad, out_weight_grad, in_bias_grad, out_bias_grad)


def solution(mesh):
    links = Links(mesh.shape["row"], mesh.shape["col"])
    in_specs = (
        P("col", "row"),
        P("row", "col"),
        P("col"),
        P("col", "row"),
        P("row"),
        P("col", "row"),
    )
    out_specs = (
        P("col", "row"),
        P("col", "row"),
        P("row", "col"),
        P("col", "row"),
        P("col"),
        P("row"),
    )

    def step(*arrays):
        return per_device(links, *arrays)

    return jax.shard_map(
        step, mesh=mesh, in_specs=in_specs, out_specs=out_specs, check_vma=False
    )
```
